32 devices in a mesh: chan: 16 (over z, y, x), tm: 2 (over core).
Axes of the slice: x: 2, y: 2, z: 4, core: 2. Of those that a mesh axis runs over, the one named last changes fastest.
Arguments:
- filterbank: bfloat16 [8, 4096, 8192], P(None, 'chan', 'tm'), may hold values from -6 to 6
- delays: int32 [12, 1024], P(None, 'chan'), may hold values from 0 to 2
- widths: int32 [8], replicated, may hold values from 1 to 128, as said below
Outputs:
- dedispersed: float32 [8, 1024, 8192], P(None, 'chan', 'tm')
- box_peaks: float32 [8, 8, 1024, 64], P(None, None, 'chan', 'tm')
The draws below stay inside these ranges and needn't reach their ends.
Inputs may be any that keep to these rules, and one draw needn't show every extreme that they name: widths[w] lies in [2^w, 2^(w+1)) for w below 7; the last equals 128.
All inputs are finite; a program needn't handle non-finite values.
Results may differ from the reference program's by a relative error of at most 0.0003.
Values sent between devices are 32-bit elements; how exact they have to be, the bound alone decides.
A program may use at most 192 MiB of HBM per device.

```python
import math
import jax
import jax.numpy as jnp
from jax import lax

SECTIONS = 12
CHANS = 4096
NDM = 1024
TILE = 128
DMAX = 2
NW = 8
BOXMAX = 128
B = 8
SAMP = 8192


def draw_widths(key, part):
    key = jax.random.fold_in(key, 11)
    powers = 2 ** jnp.arange(NW, dtype=jnp.int32)
    picked = jax.random.randint(key, (NW,), powers, 2 * powers, dtype=jnp.int32)
    return jnp.where(jnp.arange(NW) == NW - 1, BOXMAX, picked).astype(jnp.int32)


def with_ends(values, rng, least, top_value):
    index_at = [jax.random.randint(jax.random.fold_in(rng, axis), (), 0, length) for axis, length in enumerate(values.shape)]
    main_axis = values.shape.index(max(values.shape))
    next_to = index_at[:main_axis] + [(index_at[main_axis] + 1) % values.shape[main_axis]] + index_at[main_axis + 1:]
    return values.at[tuple(index_at)].set(least).at[tuple(next_to)].set(top_value)


def block_scale(key, dims, shards, least, high):
    factor_of, own = 1.0, jax.random.fold_in(key, 6)
    for axis_at, parts in shards:
        heights = jnp.exp(jax.random.uniform(jax.random.fold_in(own, axis_at), (parts,), jnp.float32, least / len(shards), high / len(shards)))
        factor_of = factor_of * jnp.repeat(heights, dims[axis_at] // parts).reshape([-1 if axis == axis_at else 1 for axis in range(len(dims))])
    return factor_of


def centred(own_key, extent, deviation, limit, pieces=(), kind=jnp.bfloat16):
    drawn = jax.random.normal(own_key, extent, jnp.float32) * deviation
    if len(pieces) > 0:
        drawn = block_scale(own_key, extent, pieces, -0.22, 0.18) * drawn
    return jnp.clip(drawn, min=-limit, max=limit).astype(kind)


def setup_inputs(seed: int = 0) -> dict:
    keys = jax.random.split(jax.random.key(seed), 4)
    return {
        "filterbank": centred(keys[0], (B, CHANS, SAMP), 1.0, 6.0, ((1, 16), (2, 2))),
        "delays": with_ends(jax.random.randint(keys[1], (SECTIONS, NDM), 0, DMAX + 1), jax.random.fold_in(keys[1], 1), 0, DMAX).astype(jnp.int32),
        "widths": draw_widths(jax.random.fold_in(keys[3], 71), 0),
    }


def delayed_rows(upper_half, shift_table):
    length = upper_half.shape[-1]
    extended = jnp.concatenate([upper_half, jnp.zeros(upper_half.shape[:-1] + (DMAX * TILE,), jnp.float32)], axis=-1)
    result = jnp.zeros(upper_half.shape, jnp.float32)
    for offset_tiles in range(DMAX + 1):
        window = extended[..., offset_tiles * TILE:offset_tiles * TILE + length]
        result = jnp.where(shift_table[..., None] == offset_tiles, window, result)
    return result

def dedisperse(spectrum, delays):
    current = spectrum.astype(jnp.float32)[:, None, :]
    for section in range(1, SECTIONS + 1):
        subbands = current.shape[0]
        trials = current.shape[1]
        new_trials = max(1, 2 ** (section - 2))
        chosen = (jnp.arange(new_trials) % trials).astype(jnp.int32)
        lower_half = current[0::2][:, chosen]
        upper_half = current[1::2][:, chosen]
        entries = (jnp.arange(subbands // 2)[:, None] * 2 ** section // 4 + jnp.arange(new_trials)[None, :]).astype(jnp.int32)
        current = lower_half + delayed_rows(upper_half, delays[section - 1][entries])
    return current[0] * jnp.float32(1.0 / math.sqrt(CHANS))

def boxcar_peaks(series, widths):
    row_count = series.shape[0]
    length = series.shape[1]
    padded = jnp.concatenate([series, jnp.zeros((row_count, 2 * BOXMAX), jnp.float32)], axis=-1)
    sums = [padded]
    for power in range(NW - 1):
        stride = 2 ** power
        previous = sums[-1]
        moved = jnp.concatenate([previous[:, stride:], jnp.zeros((row_count, stride), jnp.float32)], axis=-1)
        sums.append(previous + moved)
    peak_list = []
    for width_number in range(NW):
        span_now = widths[width_number]
        running = jnp.zeros((row_count, length), jnp.float32)
        offset = jnp.zeros((), jnp.int32)
        for power in reversed(range(NW)):
            bit_set = jnp.right_shift(span_now, power) % 2
            segment = lax.dynamic_slice_in_dim(sums[power], offset, length, axis=1)
            running = running + jnp.where(bit_set == 1, segment, jnp.float32(0.0))
            offset = (offset + bit_set * 2 ** power).astype(jnp.int32)
        scaled = running * (1.0 / jnp.sqrt(span_now.astype(jnp.float32)))
        peak_list.append(lax.optimization_barrier(jnp.max(scaled.reshape(row_count, length // TILE, TILE), axis=-1)))
    return jnp.stack(peak_list)

def reference(filterbank, delays, widths):

    def per_beam(spectrum):
        series = dedisperse(spectrum, delays)
        return (series, boxcar_peaks(series, widths))
    dedispersed, beam_peaks = lax.map(per_beam, filterbank)
    return (dedispersed, jnp.transpose(beam_peaks, (1, 0, 2, 3)))
```

```python
import functools
import math

import jax
import jax.numpy as jnp
import numpy as np
from jax import lax
from jax.experimental import pallas as pl
from jax.experimental.pallas import tpu as pltpu
from jax.sharding import PartitionSpec as P

CHANS = 4096
TILE = 128
DMAX = 2
BLOCK = 1024
MESH = pl.DeviceIdType.MESH


def table_factors(local_chans, rows):
    sections = local_chans.bit_length() - 1
    left = np.zeros((rows, sections, rows), np.float32)
    right = np.zeros((sections, rows, local_chans), np.float32)
    r = np.arange(rows)[:, None]
    j = np.arange(rows)
    c = np.arange(local_chans)[None, :]
    for section in range(1, sections + 1):
        trials = max(1, 2 ** (section - 2))
        left[:, section - 1, :] = (j[None, :] % trials) == (r % trials)
        band = c >> max(section, 2)
        upper = (c >> (section - 1)) & 1
        right[section - 1] = ((j[:, None] // trials) == band) & (upper == 1)
    return left.reshape(rows, -1), right.reshape(-1, local_chans)


def kernel(
    sizes, fb_ref, total_ref, lag_ref, width_ref, out_ref, peak_ref,
    held, rims, box_rim, spill, ext, weight, band, fb,
    send_sem, recv_sem, rim_send, rim_recv, spill_send, spill_recv, in_sem, out_sem,
):
    beams, chans, length, rows, per, merges, times = sizes
    split = rows // per
    chunks = beams * split
    tiles = length // TILE
    depth = DMAX * (chans.bit_length() - 1)
    shifts = depth + 1
    lead = depth * TILE
    rim = DMAX * TILE
    widths = width_ref.shape[0]
    me = lax.axis_index("chan")
    now = lax.axis_index("tm")
    has_left = now > 0
    has_right = now < times - 1
    left = lax.rem(now + times - 1, times)
    right = lax.rem(now + 1, times)
    is_upper = [(me // 2**m) % 2 for m in range(merges)]
    partner = [me + (1 - 2 * is_upper[m]) * 2**m for m in range(merges)]

    barrier = pltpu.get_barrier_semaphore()
    for m in range(merges):
        pl.semaphore_signal(barrier, inc=1, device_id={"chan": partner[m]}, device_id_type=MESH)

    @pl.when(has_left)
    def _():
        pl.semaphore_signal(barrier, inc=1, device_id={"tm": left}, device_id_type=MESH)

    @pl.when(has_right)
    def _():
        pl.semaphore_signal(barrier, inc=1, device_id={"tm": right}, device_id_type=MESH)

    def load(beam):
        slot = lax.rem(beam, 2)
        return pltpu.make_async_copy(fb_ref.at[beam], fb.at[slot], in_sem.at[slot])

    load(0).start()

    for q in range(split):
        total = total_ref[q * per : (q + 1) * per, :]
        for s in range(shifts):
            weight[q, s] = (total == float(s)).astype(jnp.bfloat16)
    gap = lax.broadcasted_iota(jnp.int32, (2 * TILE, TILE), 0) - lax.broadcasted_iota(jnp.int32, (2 * TILE, TILE), 1)
    for w in range(widths):
        band[:, w * TILE : (w + 1) * TILE] = ((gap >= 0) & (gap < width_ref[w])).astype(jnp.float32).astype(jnp.bfloat16)

    @pl.when(jnp.logical_not(has_right))
    def _():
        rims[...] = jnp.zeros_like(rims)
        box_rim[...] = jnp.zeros_like(box_rim)

    peers = merges + jnp.minimum(now, 1) + jnp.minimum(times - 1 - now, 1)
    pl.semaphore_wait(barrier, peers)

    def exchange(m, c):
        return pltpu.make_async_remote_copy(
            src_ref=held.at[0, c], dst_ref=held.at[m + 1, c],
            send_sem=send_sem.at[m, c], recv_sem=recv_sem.at[m, c],
            device_id={"chan": partner[m]}, device_id_type=MESH,
        )

    def rim_copy(m, c):
        slot = (1 - is_upper[m]) * (m + 1)
        return pltpu.make_async_remote_copy(
            src_ref=held.at[slot, c, :, pl.ds(0, rim)], dst_ref=rims.at[m, c],
            send_sem=rim_send.at[m, c], recv_sem=rim_recv.at[m, c],
            device_id={"tm": left}, device_id_type=MESH,
        )

    def box_copy(c):
        return pltpu.make_async_remote_copy(
            src_ref=held.at[0, c, :, pl.ds(0, TILE)], dst_ref=box_rim.at[c],
            send_sem=rim_send.at[merges, c], recv_sem=rim_recv.at[merges, c],
            device_id={"tm": left}, device_id_type=MESH,
        )

    def spill_copy(c):
        return pltpu.make_async_remote_copy(
            src_ref=ext.at[lax.rem(c, 2), :, pl.ds(0, lead)], dst_ref=spill.at[c],
            send_sem=spill_send.at[c], recv_sem=spill_recv.at[c],
            device_id={"tm": left}, device_id_type=MESH,
        )

    def place(c):
        return c // split, pl.ds(pl.multiple_of(lax.rem(c, split) * per, per), per)

    def result(c):
        beam, at = place(c)
        return pltpu.make_async_copy(held.at[0, c], out_ref.at[beam, at, :], out_sem.at[c])

    def local(c):
        beam = c // split
        q = lax.rem(c, split)
        slot = lax.rem(beam, 2)
        side = lax.rem(c, 2)

        @pl.when(q == 0)
        def _():
            load(beam).wait()

            @pl.when(beam + 1 < beams)
            def _():
                load(beam + 1).start()

        @pl.when(jnp.logical_and(has_left, c >= 2))
        def _():
            spill_copy(c - 2).wait_send()

        ext[side] = jnp.zeros(ext.shape[1:], jnp.float32)
        mat = weight[q].reshape(shifts * per, chans)
        step = BLOCK // 2

        def columns(k, carry):
            at = pl.multiple_of(k * step, step)
            part = jnp.dot(mat, fb[slot, :, pl.ds(at, step)], preferred_element_type=jnp.float32)
            for s in range(shifts):
                to = pl.ds(pl.multiple_of(at + (depth - s) * TILE, TILE), step)
                ext[side, :, to] = ext[side, :, to] + part[s * per : (s + 1) * per, :]
            return carry

        lax.fori_loop(0, length // step, columns, 0)

        @pl.when(has_left)
        def _():
            spill_copy(c).start()

        held[0, c] = ext[side, :, lead:]

    def join(c):
        @pl.when(has_right)
        def _():
            spill_copy(c).wait_recv()
            held[0, c, :, length - lead :] = held[0, c, :, length - lead :] + spill[c]

        exchange(0, c).start()

    def arrive(m, c):
        exchange(m, c).wait_recv()

        @pl.when(has_left)
        def _():
            rim_copy(m, c).start()

    def merge(m, c):
        exchange(m, c).wait_send()

        @pl.when(has_left)
        def _():
            rim_copy(m, c).wait_send()

        @pl.when(has_right)
        def _():
            rim_copy(m, c).wait_recv()

        low = is_upper[m] * (m + 1)
        high = (1 - is_upper[m]) * (m + 1)
        _, at = place(c)
        lag = jnp.concatenate([lag_ref[m, at, :]] * (BLOCK // TILE), axis=1)
        last = m == merges - 1
        for start in range(0, length, BLOCK):
            if start + BLOCK < length:
                window = held[high, c, :, start : start + BLOCK + rim]
            else:
                window = jnp.concatenate([held[high, c, :, start : start + BLOCK], rims[m, c]], axis=1)
            moved = window[:, :BLOCK]
            for offset in range(1, DMAX + 1):
                moved = jnp.where(lag == offset, window[:, offset * TILE : offset * TILE + BLOCK], moved)
            new = held[low, c, :, start : start + BLOCK] + moved
            if last:
                new = new * jnp.float32(1.0 / math.sqrt(CHANS))
            held[0, c, :, start : start + BLOCK] = new
        if last:
            result(c).start()

            @pl.when(has_left)
            def _():
                box_copy(c).start()
        else:
            exchange(m + 1, c).start()

    def peaks(c):
        @pl.when(has_right)
        def _():
            box_copy(c).wait_recv()

        beam, at = place(c)
        lane = lax.broadcasted_iota(jnp.int32, (per, TILE), 1)
        found = [jnp.zeros((per, TILE), jnp.float32) for _ in range(widths)]
        group = min(8, tiles)
        for first in range(0, tiles, group):
            start = first * TILE
            if first + group < tiles:
                window = held[0, c, :, start : start + (group + 1) * TILE]
            else:
                window = jnp.concatenate([held[0, c, :, start : start + group * TILE], box_rim[c]], axis=1)
            coarse = window.astype(jnp.bfloat16)
            fine = (window - coarse.astype(jnp.float32)).astype(jnp.bfloat16)
            pairs = [
                jnp.concatenate([part[:, i * TILE : (i + 2) * TILE] for i in range(group)], axis=0)
                for part in (coarse, fine)
            ]
            sums = sum(jnp.dot(pair, band[...], preferred_element_type=jnp.float32) for pair in pairs)
            for w in range(widths):
                best = jnp.max(sums[:, w * TILE : (w + 1) * TILE], axis=1, keepdims=True)
                for i in range(group):
                    found[w] = jnp.where(lane == first + i, best[i * per : (i + 1) * per], found[w])
        for w in range(widths):
            span = jnp.full((per, TILE), width_ref[w], jnp.int32).astype(jnp.float32)
            peak_ref[w, beam, at, :] = (found[w] * (1.0 / jnp.sqrt(span)))[:, :tiles]

    lags = [3 + 2 * m for m in range(merges)]
    lags[-1] += 1
    final = lags[-1] + 1

    def step(i, carry):
        def guarded(lag, action):
            c = i - lag

            @pl.when(jnp.logical_and(c >= 0, c < chunks))
            def _():
                action(c)

        for m in reversed(range(merges)):
            guarded(lags[m], functools.partial(arrive, m))
        guarded(1, join)
        guarded(0, local)
        for m in reversed(range(merges)):
            guarded(lags[m], functools.partial(merge, m))
        guarded(final, peaks)
        return carry

    lax.fori_loop(0, chunks + final, step, 0)

    def drain(c, carry):
        result(c).wait()

        @pl.when(has_left)
        def _():
            box_copy(c).wait_send()

            @pl.when(c >= chunks - 2)
            def _():
                spill_copy(c).wait_send()

        return carry

    lax.fori_loop(0, chunks, drain, 0)


def shards(filterbank, delays, widths):
    beams, chans, length = filterbank.shape
    rows = chans // 4
    per = min(rows, 16)
    chunks = beams * (rows // per)
    local_sections = chans.bit_length() - 1
    merges = lax.axis_size("chan").bit_length() - 1
    times = lax.axis_size("tm")
    tiles = length // TILE
    depth = DMAX * local_sections
    left, right = table_factors(chans, rows)
    table = delays[:local_sections].reshape(-1, 1).astype(jnp.bfloat16) * jnp.asarray(right, jnp.bfloat16)
    total = jnp.dot(jnp.asarray(left, jnp.bfloat16), table, preferred_element_type=jnp.float32)
    lag = jnp.broadcast_to(delays[local_sections:, :, None], (merges, rows, TILE))
    sizes = (beams, chans, length, rows, per, merges, times)
    f32 = jnp.float32
    vmem = pl.BlockSpec(memory_space=pltpu.VMEM)
    hbm = pl.BlockSpec(memory_space=pl.ANY)
    dma = pltpu.SemaphoreType.DMA
    return pl.pallas_call(
        functools.partial(kernel, sizes),
        out_shape=(
            jax.ShapeDtypeStruct((beams, rows, length), f32),
            jax.ShapeDtypeStruct((widths.shape[0], beams, rows, tiles), f32),
        ),
        in_specs=[hbm, vmem, vmem, pl.BlockSpec(memory_space=pltpu.SMEM)],
        out_specs=(hbm, vmem),
        scratch_shapes=[
            pltpu.VMEM((merges + 1, chunks, per, length), f32),
            pltpu.VMEM((merges, chunks, per, DMAX * TILE), f32),
            pltpu.VMEM((chunks, per, TILE), f32),
            pltpu.VMEM((chunks, per, depth * TILE), f32),
            pltpu.VMEM((2, per, depth * TILE + length), f32),
            pltpu.VMEM((rows // per, depth + 1, per, chans), jnp.bfloat16),
            pltpu.VMEM((2 * TILE, widths.shape[0] * TILE), jnp.bfloat16),
            pltpu.VMEM((2, chans, length), jnp.bfloat16),
            dma((merges, chunks)),
            dma((merges, chunks)),
            dma((merges + 1, chunks)),
            dma((merges + 1, chunks)),
            dma((chunks,)),
            dma((chunks,)),
            dma((2,)),
            dma((chunks,)),
        ],
        compiler_params=pltpu.CompilerParams(
            collective_id=0, has_side_effects=True, vmem_limit_bytes=60 * 2**20
        ),
        name="dedisperse",
    )(filterbank, total, lag, widths)


def solution(mesh):
    return jax.shard_map(
        shards,
        mesh=mesh,
        in_specs=(P(None, "chan", "tm"), P(None, "chan"), P()),
        out_specs=(P(None, "chan", "tm"), P(None, None, "chan", "tm")),
        check_vma=False,
    )
```

```python
import functools
import math

import jax
import jax.numpy as jnp
from jax import lax
from jax.experimental import pallas as pl
from jax.experimental.pallas import tpu as pltpu
from jax.sharding import PartitionSpec as P

CHANS = 4096
TILE = 128
DMAX = 2
BLOCK = 1024
MESH = pl.DeviceIdType.MESH


def kernel(
    sizes, fb_ref, delay_ref, width_ref, out_ref, peak_ref,
    held, rims, box_rim, spill, ext, weight, lags_of, band, fb,
    send_sem, recv_sem, rim_send, rim_recv, spill_send, spill_recv, in_sem, out_sem,
):
    beams, chans, length, rows, per, merges, times = sizes
    split = rows // per
    chunks = beams * split
    tiles = length // TILE
    depth = DMAX * (chans.bit_length() - 1)
    shifts = depth + 1
    lead = depth * TILE
    rim = DMAX * TILE
    widths = width_ref.shape[0]
    me = lax.axis_index("chan")
    now = lax.axis_index("tm")
    has_left = now > 0
    has_right = now < times - 1
    left = lax.rem(now + times - 1, times)
    right = lax.rem(now + 1, times)
    is_upper = [(me // 2**m) % 2 for m in range(merges)]
    partner = [me + (1 - 2 * is_upper[m]) * 2**m for m in range(merges)]

    barrier = pltpu.get_barrier_semaphore()
    for m in range(merges):
        pl.semaphore_signal(barrier, inc=1, device_id={"chan": partner[m]}, device_id_type=MESH)

    @pl.when(has_left)
    def _():
        pl.semaphore_signal(barrier, inc=1, device_id={"tm": left}, device_id_type=MESH)

    @pl.when(has_right)
    def _():
        pl.semaphore_signal(barrier, inc=1, device_id={"tm": right}, device_id_type=MESH)

    def load(beam):
        slot = lax.rem(beam, 2)
        return pltpu.make_async_copy(fb_ref.at[beam], fb.at[slot], in_sem.at[slot])

    load(0).start()

    sections = chans.bit_length() - 1
    grid = lambda shape, axis: lax.broadcasted_iota(jnp.int32, shape, axis)
    flag = lambda test: jnp.where(test, 1.0, 0.0)
    total = jnp.zeros((rows, chans), jnp.float32)
    for section in range(1, sections + 1):
        trials = max(1, 2 ** (section - 2))
        entry, trial = grid((rows, rows), 1), grid((rows, rows), 0)
        same = flag((entry & (trials - 1)) == (trial & (trials - 1)))
        picked = same * delay_ref[section - 1 : section, :].astype(jnp.float32)
        entry, chan = grid((rows, chans), 0), grid((rows, chans), 1)
        band_of = lax.shift_right_logical(entry, max(section, 2) - 2) == lax.shift_right_logical(chan, max(section, 2))
        upper = (lax.shift_right_logical(chan, section - 1) & 1) == 1
        total = total + jnp.dot(
            picked.astype(jnp.bfloat16), flag(band_of & upper).astype(jnp.bfloat16), preferred_element_type=jnp.float32
        )
    for q in range(split):
        part = total[q * per : (q + 1) * per, :]
        for s in range(0, shifts, 2):
            pair = jnp.concatenate([flag(part == float(s)), flag(part == float(s + 1))], axis=0)
            weight[q, s * per : (s + 2) * per, :] = pair.astype(jnp.bfloat16)
    own = flag(grid((rows, rows), 0) == grid((rows, rows), 1))
    for m in range(merges):
        picked = own * delay_ref[sections + m : sections + m + 1, :].astype(jnp.float32)
        lags_of[m] = jnp.dot(
            picked.astype(jnp.bfloat16), jnp.ones((rows, TILE), jnp.bfloat16), preferred_element_type=jnp.float32
        )
    gap = lax.broadcasted_iota(jnp.int32, (2 * TILE, TILE), 0) - lax.broadcasted_iota(jnp.int32, (2 * TILE, TILE), 1)
    for w in range(widths):
        band[:, w * TILE : (w + 1) * TILE] = ((gap >= 0) & (gap < width_ref[w])).astype(jnp.float32).astype(jnp.bfloat16)

    @pl.when(jnp.logical_not(has_right))
    def _():
        rims[...] = jnp.zeros_like(rims)
        box_rim[...] = jnp.zeros_like(box_rim)

    peers = merges + jnp.minimum(now, 1) + jnp.minimum(times - 1 - now, 1)
    pl.semaphore_wait(barrier, peers)

    def exchange(m, c):
        return pltpu.make_async_remote_copy(
            src_ref=held.at[0, c], dst_ref=held.at[m + 1, c],
            send_sem=send_sem.at[m, c], recv_sem=recv_sem.at[m, c],
            device_id={"chan": partner[m]}, device_id_type=MESH,
        )

    def rim_copy(m, c):
        slot = (1 - is_upper[m]) * (m + 1)
        return pltpu.make_async_remote_copy(
            src_ref=held.at[slot, c, :, pl.ds(0, rim)], dst_ref=rims.at[m, c],
            send_sem=rim_send.at[m, c], recv_sem=rim_recv.at[m, c],
            device_id={"tm": left}, device_id_type=MESH,
        )

    def box_copy(c):
        return pltpu.make_async_remote_copy(
            src_ref=held.at[0, c, :, pl.ds(0, TILE)], dst_ref=box_rim.at[c],
            send_sem=rim_send.at[merges, c], recv_sem=rim_recv.at[merges, c],
            device_id={"tm": left}, device_id_type=MESH,
        )

    def spill_copy(c):
        return pltpu.make_async_remote_copy(
            src_ref=ext.at[lax.rem(c, 2), :, pl.ds(0, lead)], dst_ref=spill.at[c],
            send_sem=spill_send.at[c], recv_sem=spill_recv.at[c],
            device_id={"tm": left}, device_id_type=MESH,
        )

    def place(c):
        return c // split, pl.ds(pl.multiple_of(lax.rem(c, split) * per, per), per)

    def result(c):
        beam, at = place(c)
        return pltpu.make_async_copy(held.at[0, c], out_ref.at[beam, at, :], out_sem.at[c])

    def local(c):
        beam = c // split
        q = lax.rem(c, split)
        slot = lax.rem(beam, 2)
        side = lax.rem(c, 2)

        @pl.when(q == 0)
        def _():
            load(beam).wait()

            @pl.when(beam + 1 < beams)
            def _():
                load(beam + 1).start()

        @pl.when(jnp.logical_and(has_left, c >= 2))
        def _():
            spill_copy(c - 2).wait_send()

        ext[side] = jnp.zeros(ext.shape[1:], jnp.float32)
        mat = weight[q]
        step = BLOCK // 2

        def columns(k, carry):
            at = pl.multiple_of(k * step, step)
            part = jnp.dot(mat, fb[slot, :, pl.ds(at, step)], preferred_element_type=jnp.float32)
            for s in range(shifts):
                to = pl.ds(pl.multiple_of(at + (depth - s) * TILE, TILE), step)
                ext[side, :, to] = ext[side, :, to] + part[s * per : (s + 1) * per, :]
            return carry

        lax.fori_loop(0, length // step, columns, 0, unroll=2)

        @pl.when(has_left)
        def _():
            spill_copy(c).start()

        held[0, c] = ext[side, :, lead:]

    def join(c):
        @pl.when(has_right)
        def _():
            spill_copy(c).wait_recv()
            held[0, c, :, length - lead :] = held[0, c, :, length - lead :] + spill[c]

        exchange(0, c).start()

    def arrive(m, c):
        exchange(m, c).wait_recv()

        @pl.when(has_left)
        def _():
            rim_copy(m, c).start()

    def merge(m, c):
        exchange(m, c).wait_send()

        @pl.when(has_left)
        def _():
            rim_copy(m, c).wait_send()

        @pl.when(has_right)
        def _():
            rim_copy(m, c).wait_recv()

        low = is_upper[m] * (m + 1)
        high = (1 - is_upper[m]) * (m + 1)
        _, at = place(c)
        lag = jnp.concatenate([lags_of[m, at, :]] * (BLOCK // TILE), axis=1)
        last = m == merges - 1
        for start in range(0, length, BLOCK):
            if start + BLOCK < length:
                window = held[high, c, :, start : start + BLOCK + rim]
            else:
                window = jnp.concatenate([held[high, c, :, start : start + BLOCK], rims[m, c]], axis=1)
            moved = window[:, :BLOCK]
            for offset in range(1, DMAX + 1):
                moved = jnp.where(lag == float(offset), window[:, offset * TILE : offset * TILE + BLOCK], moved)
            new = held[low, c, :, start : start + BLOCK] + moved
            if last:
                new = new * jnp.float32(1.0 / math.sqrt(CHANS))
            held[0, c, :, start : start + BLOCK] = new
        if last:
            result(c).start()

            @pl.when(has_left)
            def _():
                box_copy(c).start()
        else:
            exchange(m + 1, c).start()

    def peaks(c):
        @pl.when(has_right)
        def _():
            box_copy(c).wait_recv()

        beam, at = place(c)
        lane = lax.broadcasted_iota(jnp.int32, (per, TILE), 1)
        found = [jnp.zeros((per, TILE), jnp.float32) for _ in range(widths)]
        group = min(16, tiles)
        for first in range(0, tiles, group):
            start = first * TILE
            if first + group < tiles:
                window = held[0, c, :, start : start + (group + 1) * TILE]
            else:
                window = jnp.concatenate([held[0, c, :, start : start + group * TILE], box_rim[c]], axis=1)
            pairs = jnp.concatenate([window[:, i * TILE : (i + 2) * TILE] for i in range(group)], axis=0)
            coarse = pairs.astype(jnp.bfloat16)
            fine = (pairs - coarse.astype(jnp.float32)).astype(jnp.bfloat16)
            both = jnp.concatenate([coarse, fine], axis=0)
            sums = jnp.dot(both, band[...], preferred_element_type=jnp.float32)
            sums = sums[: group * per] + sums[group * per :]
            for w in range(widths):
                best = jnp.max(sums[:, w * TILE : (w + 1) * TILE], axis=1, keepdims=True)
                for i in range(group):
                    found[w] = jnp.where(lane == first + i, best[i * per : (i + 1) * per], found[w])
        for w in range(widths):
            span = jnp.full((per, TILE), width_ref[w], jnp.int32).astype(jnp.float32)
            peak_ref[w, beam, at, :] = (found[w] * (1.0 / jnp.sqrt(span)))[:, :tiles]

    lags = [3 + 2 * m for m in range(merges)]
    lags[-1] += 3
    final = lags[-1] + 1

    def step(i, carry):
        def guarded(lag, action):
            c = i - lag

            @pl.when(jnp.logical_and(c >= 0, c < chunks))
            def _():
                action(c)

        for m in reversed(range(merges)):
            guarded(lags[m], functools.partial(arrive, m))
        guarded(1, join)
        guarded(0, local)
        for m in reversed(range(merges)):
            guarded(lags[m], functools.partial(merge, m))
        guarded(final, peaks)
        return carry

    lax.fori_loop(0, chunks + final, step, 0)

    def drain(c, carry):
        result(c).wait()

        @pl.when(has_left)
        def _():
            box_copy(c).wait_send()

            @pl.when(c >= chunks - 2)
            def _():
                spill_copy(c).wait_send()

        return carry

    lax.fori_loop(0, chunks, drain, 0)


def hand_over(series_ref, peak_ref, series_out, peak_out, sems):
    widths, beams = peak_ref.shape[:2]
    copies = [pltpu.make_async_copy(series_ref.at[b], series_out.at[b], sems.at[b]) for b in range(beams)]
    for copy in copies:
        copy.start()

    def turn(b, carry):
        for w in range(widths):
            peak_out[w, b] = peak_ref[w, b].T
        return carry

    lax.fori_loop(0, beams, turn, 0)
    for copy in copies:
        copy.wait()


def shards(filterbank, delays, widths):
    beams, chans, length = filterbank.shape
    rows = chans // 4
    per = 8
    chunks = beams * (rows // per)
    local_sections = chans.bit_length() - 1
    merges = lax.axis_size("chan").bit_length() - 1
    times = lax.axis_size("tm")
    tiles = length // TILE
    depth = DMAX * local_sections
    stacked = (depth // 2 + 1) * 2 * per
    sizes = (beams, chans, length, rows, per, merges, times)
    f32 = jnp.float32
    vmem = pl.BlockSpec(memory_space=pltpu.VMEM)
    hbm = pl.BlockSpec(memory_space=pl.ANY)
    dma = pltpu.SemaphoreType.DMA
    shapes = (
        jax.ShapeDtypeStruct((beams, rows, length), f32),
        jax.ShapeDtypeStruct((widths.shape[0], beams, rows, tiles), f32),
    )
    results = pl.pallas_call(
        functools.partial(kernel, sizes),
        out_shape=shapes,
        in_specs=[hbm, vmem, pl.BlockSpec(memory_space=pltpu.SMEM)],
        out_specs=(hbm, vmem),
        scratch_shapes=[
            pltpu.VMEM((merges + 1, chunks, per, length), f32),
            pltpu.VMEM((merges, chunks, per, DMAX * TILE), f32),
            pltpu.VMEM((chunks, per, TILE), f32),
            pltpu.VMEM((chunks, per, depth * TILE), f32),
            pltpu.VMEM((2, per, depth * TILE + length), f32),
            pltpu.VMEM((rows // per, stacked, chans), jnp.bfloat16),
            pltpu.VMEM((merges, rows, TILE), f32),
            pltpu.VMEM((2 * TILE, widths.shape[0] * TILE), jnp.bfloat16),
            pltpu.VMEM((2, chans, length), jnp.bfloat16),
            dma((merges, chunks)),
            dma((merges, chunks)),
            dma((merges + 1, chunks)),
            dma((merges + 1, chunks)),
            dma((chunks,)),
            dma((chunks,)),
            dma((2,)),
            dma((chunks,)),
        ],
        compiler_params=pltpu.CompilerParams(
            collective_id=0, has_side_effects=True, vmem_limit_bytes=60 * 2**20
        ),
        name="dedisperse",
    )(filterbank, delays, widths)
    turned = (widths.shape[0], beams, tiles, rows)
    series, peaks = pl.pallas_call(
        hand_over,
        out_shape=(shapes[0], jax.ShapeDtypeStruct(turned, f32)),
        in_specs=[hbm, vmem],
        out_specs=(hbm, vmem),
        scratch_shapes=[dma((beams,))],
        compiler_params=pltpu.CompilerParams(vmem_limit_bytes=60 * 2**20),
        name="hand_over",
    )(*results)
    return series, jnp.swapaxes(peaks, 2, 3)


def solution(mesh):
    return jax.shard_map(
        shards,
        mesh=mesh,
        in_specs=(P(None, "chan", "tm"), P(None, "chan"), P()),
        out_specs=(P(None, "chan", "tm"), P(None, None, "chan", "tm")),
        check_vma=False,
    )
```

```python
import functools
import math

import jax
import jax.numpy as jnp
from jax import lax
from jax.experimental import pallas as pl
from jax.experimental.pallas import tpu as pltpu
from jax.sharding import PartitionSpec as P

CHANS = 4096
TILE = 128
DMAX = 2
BLOCK = 16
MESH = pl.DeviceIdType.MESH


def kernel(
    sizes, fb_ref, delay_ref, width_ref, out_ref, peak_ref,
    held, rims, box_rim, spill, ext, weight, lags_of, band, fb,
    send_sem, recv_sem, rim_send, rim_recv, spill_send, spill_recv, in_sem, out_sem,
):
    beams, chans, length, rows, per, merges, times = sizes
    split = rows // per
    chunks = beams * split
    tiles = length // TILE
    depth = DMAX * (chans.bit_length() - 1)
    shifts = depth + 1
    widths = width_ref.shape[0]
    me = lax.axis_index("chan")
    now = lax.axis_index("tm")
    has_left = now > 0
    has_right = now < times - 1
    left = lax.rem(now + times - 1, times)
    right = lax.rem(now + 1, times)
    is_upper = [(me // 2**m) % 2 for m in range(merges)]
    partner = [me + (1 - 2 * is_upper[m]) * 2**m for m in range(merges)]

    barrier = pltpu.get_barrier_semaphore()
    for m in range(merges):
        pl.semaphore_signal(barrier, inc=1, device_id={"chan": partner[m]}, device_id_type=MESH)

    @pl.when(has_left)
    def _():
        pl.semaphore_signal(barrier, inc=1, device_id={"tm": left}, device_id_type=MESH)

    @pl.when(has_right)
    def _():
        pl.semaphore_signal(barrier, inc=1, device_id={"tm": right}, device_id_type=MESH)

    def load(beam):
        slot = lax.rem(beam, 2)
        return pltpu.make_async_copy(fb_ref.at[beam], fb.at[slot], in_sem.at[slot])

    load(0).start()

    sections = chans.bit_length() - 1
    grid = lambda shape, axis: lax.broadcasted_iota(jnp.int32, shape, axis)
    flag = lambda test: jnp.where(test, 1.0, 0.0)
    total = jnp.zeros((rows, chans), jnp.float32)
    for section in range(1, sections + 1):
        trials = max(1, 2 ** (section - 2))
        entry, trial = grid((rows, rows), 1), grid((rows, rows), 0)
        same = flag((entry & (trials - 1)) == (trial & (trials - 1)))
        picked = same * delay_ref[section - 1 : section, :].astype(jnp.float32)
        entry, chan = grid((rows, chans), 0), grid((rows, chans), 1)
        band_of = lax.shift_right_logical(entry, max(section, 2) - 2) == lax.shift_right_logical(chan, max(section, 2))
        upper = (lax.shift_right_logical(chan, section - 1) & 1) == 1
        total = total + jnp.dot(
            picked.astype(jnp.bfloat16), flag(band_of & upper).astype(jnp.bfloat16), preferred_element_type=jnp.float32
        )
    for q in range(split):
        part = total[q * per : (q + 1) * per, :]
        for p in range(0, shifts, 2):
            s = depth - p
            pair = jnp.concatenate([flag(part == float(s)), flag(part == float(s - 1))], axis=0)
            weight[q, p * per : (p + 2) * per, :] = pair.astype(jnp.bfloat16)
    own = flag(grid((rows, rows), 0) == grid((rows, rows), 1))
    for m in range(merges):
        picked = own * delay_ref[sections + m : sections + m + 1, :].astype(jnp.float32)
        lags_of[m] = jnp.dot(
            picked.astype(jnp.bfloat16), jnp.ones((rows, TILE), jnp.bfloat16), preferred_element_type=jnp.float32
        )
    gap = lax.broadcasted_iota(jnp.int32, (2 * TILE, TILE), 0) - lax.broadcasted_iota(jnp.int32, (2 * TILE, TILE), 1)
    for w in range(widths):
        band[:, w * TILE : (w + 1) * TILE] = ((gap >= 0) & (gap < width_ref[w])).astype(jnp.float32).astype(jnp.bfloat16)

    @pl.when(jnp.logical_not(has_right))
    def _():
        rims[...] = jnp.zeros_like(rims)
        box_rim[...] = jnp.zeros_like(box_rim)

    peers = merges + jnp.minimum(now, 1) + jnp.minimum(times - 1 - now, 1)
    pl.semaphore_wait(barrier, peers)

    def exchange(m, c):
        return pltpu.make_async_remote_copy(
            src_ref=held.at[0, c], dst_ref=held.at[m + 1, c],
            send_sem=send_sem.at[m, c], recv_sem=recv_sem.at[m, c],
            device_id={"chan": partner[m]}, device_id_type=MESH,
        )

    def rim_copy(m, c):
        slot = (1 - is_upper[m]) * (m + 1)
        return pltpu.make_async_remote_copy(
            src_ref=held.at[slot, c, pl.ds(0, DMAX)], dst_ref=rims.at[m, c],
            send_sem=rim_send.at[m, c], recv_sem=rim_recv.at[m, c],
            device_id={"tm": left}, device_id_type=MESH,
        )

    def box_copy(c):
        return pltpu.make_async_remote_copy(
            src_ref=held.at[0, c, pl.ds(0, 1)], dst_ref=box_rim.at[c],
            send_sem=rim_send.at[merges, c], recv_sem=rim_recv.at[merges, c],
            device_id={"tm": left}, device_id_type=MESH,
        )

    def spill_copy(c):
        return pltpu.make_async_remote_copy(
            src_ref=ext.at[lax.rem(c, 2), pl.ds(0, depth)], dst_ref=spill.at[c],
            send_sem=spill_send.at[c], recv_sem=spill_recv.at[c],
            device_id={"tm": left}, device_id_type=MESH,
        )

    def place(c):
        return c // split, pl.ds(pl.multiple_of(lax.rem(c, split) * per, per), per)

    def result(c):
        return pltpu.make_async_copy(held.at[0, c], out_ref.at[c // split, lax.rem(c, split)], out_sem.at[c])

    def local(c):
        beam = c // split
        q = lax.rem(c, split)
        slot = lax.rem(beam, 2)
        side = lax.rem(c, 2)

        @pl.when(q == 0)
        def _():
            load(beam).wait()

            @pl.when(beam + 1 < beams)
            def _():
                load(beam + 1).start()

        @pl.when(jnp.logical_and(has_left, c >= 2))
        def _():
            spill_copy(c - 2).wait_send()

        ext[side] = jnp.zeros(ext.shape[1:], jnp.float32)
        mat = weight[q]
        group = 4

        def columns(k, carry):
            at = pl.multiple_of(k * (group * TILE), group * TILE)
            part = jnp.dot(mat, fb[slot, :, pl.ds(at, group * TILE)], preferred_element_type=jnp.float32)
            sums = []
            for j in range(group):
                block = part[: shifts * per, j * TILE : (j + 1) * TILE].reshape(shifts, per, TILE)
                ends = [jnp.zeros((n, per, TILE), jnp.float32) for n in (j, group - 1 - j) if n > 0]
                if j > 0:
                    block = jnp.concatenate([ends[0], block], axis=0)
                if j < group - 1:
                    block = jnp.concatenate([block, ends[-1]], axis=0)
                sums.append(block)
            to = pl.ds(k * group, depth + group)
            ext[side, to] = ext[side, to] + ((sums[0] + sums[1]) + (sums[2] + sums[3]))
            return carry

        lax.fori_loop(0, tiles // group, columns, 0, unroll=2)

        @pl.when(has_left)
        def _():
            spill_copy(c).start()

        held[0, c] = ext[side, depth:]

    def join(c):
        @pl.when(has_right)
        def _():
            spill_copy(c).wait_recv()
            held[0, c, tiles - depth :] = held[0, c, tiles - depth :] + spill[c]

        exchange(0, c).start()

    def arrive(m, c):
        exchange(m, c).wait_recv()

        @pl.when(has_left)
        def _():
            rim_copy(m, c).start()

    def merge(m, c):
        exchange(m, c).wait_send()

        @pl.when(has_left)
        def _():
            rim_copy(m, c).wait_send()

        @pl.when(has_right)
        def _():
            rim_copy(m, c).wait_recv()

        low = is_upper[m] * (m + 1)
        high = (1 - is_upper[m]) * (m + 1)
        _, at = place(c)
        lag = lags_of[m, at, :][None]
        last = m == merges - 1
        for start in range(0, tiles, BLOCK):
            end = start + BLOCK
            if end < tiles:
                window = held[high, c, start : end + DMAX]
            else:
                window = jnp.concatenate([held[high, c, start:end], rims[m, c]], axis=0)
            moved = window[:BLOCK]
            for offset in range(1, DMAX + 1):
                moved = jnp.where(lag == float(offset), window[offset : offset + BLOCK], moved)
            new = held[low, c, start:end] + moved
            if last:
                new = new * jnp.float32(1.0 / math.sqrt(CHANS))
            held[0, c, start:end] = new
        if last:
            result(c).start()

            @pl.when(has_left)
            def _():
                box_copy(c).start()
        else:
            exchange(m + 1, c).start()

    def peaks(c):
        @pl.when(has_right)
        def _():
            box_copy(c).wait_recv()

        beam, at = place(c)
        lane = lax.broadcasted_iota(jnp.int32, (per, TILE), 1)
        found = [jnp.zeros((per, TILE), jnp.float32) for _ in range(widths)]
        group = min(16, tiles)
        for first in range(0, tiles, group):
            if first + group < tiles:
                window = held[0, c, first : first + group + 1]
            else:
                window = jnp.concatenate([held[0, c, first : first + group], box_rim[c]], axis=0)
            pairs = jnp.concatenate([window[:group], window[1:]], axis=2).reshape(group * per, 2 * TILE)
            coarse = pairs.astype(jnp.bfloat16)
            fine = (pairs - coarse.astype(jnp.float32)).astype(jnp.bfloat16)
            both = jnp.concatenate([coarse, fine], axis=0)
            sums = jnp.dot(both, band[...], preferred_element_type=jnp.float32)
            sums = sums[: group * per] + sums[group * per :]
            for w in range(widths):
                best = jnp.max(sums[:, w * TILE : (w + 1) * TILE], axis=1, keepdims=True)
                for i in range(group):
                    found[w] = jnp.where(lane == first + i, best[i * per : (i + 1) * per], found[w])
        for w in range(widths):
            span = jnp.full((per, TILE), width_ref[w], jnp.int32).astype(jnp.float32)
            peak_ref[w, beam, at, :] = (found[w] * (1.0 / jnp.sqrt(span)))[:, :tiles]

    lags = [3 + 2 * m for m in range(merges)]
    lags[-1] += 3
    final = lags[-1] + 1

    def step(i, carry):
        def guarded(lag, action):
            c = i - lag

            @pl.when(jnp.logical_and(c >= 0, c < chunks))
            def _():
                action(c)

        for m in reversed(range(merges)):
            guarded(lags[m], functools.partial(arrive, m))
        guarded(1, join)
        guarded(0, local)
        for m in reversed(range(merges)):
            guarded(lags[m], functools.partial(merge, m))
        guarded(final, peaks)
        return carry

    lax.fori_loop(0, chunks + final, step, 0)

    def drain(c, carry):
        result(c).wait()

        @pl.when(has_left)
        def _():
            box_copy(c).wait_send()

            @pl.when(c >= chunks - 2)
            def _():
                spill_copy(c).wait_send()

        return carry

    lax.fori_loop(0, chunks, drain, 0)


def hand_over(series_ref, peak_ref, series_out, peak_out):
    _, split, tiles, per, _ = series_ref.shape
    for i in range(tiles):
        for q in range(split):
            series_out[0, q * per : (q + 1) * per, i * TILE : (i + 1) * TILE] = series_ref[0, q, i]
    for w in range(peak_ref.shape[0]):
        peak_out[w, 0] = peak_ref[w, 0].T


def shards(filterbank, delays, widths):
    beams, chans, length = filterbank.shape
    rows = chans // 4
    per = 8
    chunks = beams * (rows // per)
    local_sections = chans.bit_length() - 1
    merges = lax.axis_size("chan").bit_length() - 1
    times = lax.axis_size("tm")
    tiles = length // TILE
    depth = DMAX * local_sections
    stacked = (depth // 2 + 1) * 2 * per
    sizes = (beams, chans, length, rows, per, merges, times)
    f32 = jnp.float32
    vmem = pl.BlockSpec(memory_space=pltpu.VMEM)
    hbm = pl.BlockSpec(memory_space=pl.ANY)
    dma = pltpu.SemaphoreType.DMA
    split = rows // per
    spans = widths.shape[0]
    shapes = (
        jax.ShapeDtypeStruct((beams, split, tiles, per, TILE), f32),
        jax.ShapeDtypeStruct((spans, beams, rows, tiles), f32),
    )
    results = pl.pallas_call(
        functools.partial(kernel, sizes),
        out_shape=shapes,
        in_specs=[hbm, vmem, pl.BlockSpec(memory_space=pltpu.SMEM)],
        out_specs=(hbm, vmem),
        scratch_shapes=[
            pltpu.VMEM((merges + 1, chunks, tiles, per, TILE), f32),
            pltpu.VMEM((merges, chunks, DMAX, per, TILE), f32),
            pltpu.VMEM((chunks, 1, per, TILE), f32),
            pltpu.VMEM((chunks, depth, per, TILE), f32),
            pltpu.VMEM((2, depth + tiles, per, TILE), f32),
            pltpu.VMEM((rows // per, stacked, chans), jnp.bfloat16),
            pltpu.VMEM((merges, rows, TILE), f32),
            pltpu.VMEM((2 * TILE, widths.shape[0] * TILE), jnp.bfloat16),
            pltpu.VMEM((2, chans, length), jnp.bfloat16),
            dma((merges, chunks)),
            dma((merges, chunks)),
            dma((merges + 1, chunks)),
            dma((merges + 1, chunks)),
            dma((chunks,)),
            dma((chunks,)),
            dma((2,)),
            dma((chunks,)),
        ],
        compiler_params=pltpu.CompilerParams(
            collective_id=0, has_side_effects=True, vmem_limit_bytes=60 * 2**20
        ),
        name="dedisperse",
    )(filterbank, delays, widths)
    series, peaks = pl.pallas_call(
        hand_over,
        grid=(beams,),
        out_shape=(
            jax.ShapeDtypeStruct((beams, rows, length), f32),
            jax.ShapeDtypeStruct((spans, beams, tiles, rows), f32),
        ),
        in_specs=[
            pl.BlockSpec((1, split, tiles, per, TILE), lambda b: (b, 0, 0, 0, 0)),
            pl.BlockSpec((spans, 1, rows, tiles), lambda b: (0, b, 0, 0)),
        ],
        out_specs=(
            pl.BlockSpec((1, rows, length), lambda b: (b, 0, 0)),
            pl.BlockSpec((spans, 1, tiles, rows), lambda b: (0, b, 0, 0)),
        ),
        compiler_params=pltpu.CompilerParams(vmem_limit_bytes=60 * 2**20),
        name="hand_over",
    )(*results)
    return series, jnp.swapaxes(peaks, 2, 3)


def solution(mesh):
    return jax.shard_map(
        shards,
        mesh=mesh,
        in_specs=(P(None, "chan", "tm"), P(None, "chan"), P()),
        out_specs=(P(None, "chan", "tm"), P(None, None, "chan", "tm")),
        check_vma=False,
    )
```

```python
import functools
import math

import jax
import jax.numpy as jnp
from jax import lax
from jax.experimental import pallas as pl
from jax.experimental.pallas import tpu as pltpu
from jax.sharding import PartitionSpec as P

CHANS = 4096
TILE = 128
DMAX = 2
BLOCK = 16
MESH = pl.DeviceIdType.MESH


def kernel(
    sizes, fb_ref, delay_ref, width_ref, out_ref, peak_ref,
    held, rims, box_rim, spill, ext, weight, lags_of, band, fb,
    send_sem, recv_sem, rim_send, rim_recv, spill_send, spill_recv, in_sem, out_sem,
):
    beams, chans, length, rows, per, merges, times = sizes
    split = rows // per
    chunks = beams * split
    tiles = length // TILE
    depth = DMAX * (chans.bit_length() - 1)
    shifts = depth + 1
    widths = width_ref.shape[0]
    me = lax.axis_index("chan")
    now = lax.axis_index("tm")
    has_left = now > 0
    has_right = now < times - 1
    left = lax.rem(now + times - 1, times)
    right = lax.rem(now + 1, times)
    is_upper = [(me // 2**m) % 2 for m in range(merges)]
    partner = [me + (1 - 2 * is_upper[m]) * 2**m for m in range(merges)]

    barrier = pltpu.get_barrier_semaphore()
    for m in range(merges):
        pl.semaphore_signal(barrier, inc=1, device_id={"chan": partner[m]}, device_id_type=MESH)

    @pl.when(has_left)
    def _():
        pl.semaphore_signal(barrier, inc=1, device_id={"tm": left}, device_id_type=MESH)

    @pl.when(has_right)
    def _():
        pl.semaphore_signal(barrier, inc=1, device_id={"tm": right}, device_id_type=MESH)

    def load(beam):
        slot = lax.rem(beam, 2)
        return pltpu.make_async_copy(fb_ref.at[beam], fb.at[slot], in_sem.at[slot])

    load(0).start()

    sections = chans.bit_length() - 1
    grid = lambda shape, axis: lax.broadcasted_iota(jnp.int32, shape, axis)
    flag = lambda test: jnp.where(test, 1.0, 0.0)
    total = jnp.zeros((rows, chans), jnp.float32)
    for section in range(1, sections + 1):
        trials = max(1, 2 ** (section - 2))
        entry, trial = grid((rows, rows), 1), grid((rows, rows), 0)
        same = flag((entry & (trials - 1)) == (trial & (trials - 1)))
        picked = same * delay_ref[section - 1 : section, :].astype(jnp.float32)
        entry, chan = grid((rows, chans), 0), grid((rows, chans), 1)
        band_of = lax.shift_right_logical(entry, max(section, 2) - 2) == lax.shift_right_logical(chan, max(section, 2))
        upper = (lax.shift_right_logical(chan, section - 1) & 1) == 1
        total = total + jnp.dot(
            picked.astype(jnp.bfloat16), flag(band_of & upper).astype(jnp.bfloat16), preferred_element_type=jnp.float32
        )
    for q in range(split):
        part = total[q * per : (q + 1) * per, :]
        for p in range(0, shifts, 2):
            s = depth - p
            pair = jnp.concatenate([flag(part == float(s)), flag(part == float(s - 1))], axis=0)
            weight[q, p * per : (p + 2) * per, :] = pair.astype(jnp.bfloat16)
    own = flag(grid((rows, rows), 0) == grid((rows, rows), 1))
    for m in range(merges):
        picked = own * delay_ref[sections + m : sections + m + 1, :].astype(jnp.float32)
        lags_of[m] = jnp.dot(
            picked.astype(jnp.bfloat16), jnp.ones((rows, TILE), jnp.bfloat16), preferred_element_type=jnp.float32
        )
    gap = lax.broadcasted_iota(jnp.int32, (2 * TILE, TILE), 0) - lax.broadcasted_iota(jnp.int32, (2 * TILE, TILE), 1)
    for w in range(widths):
        band[:, w * TILE : (w + 1) * TILE] = ((gap >= 0) & (gap < width_ref[w])).astype(jnp.float32).astype(jnp.bfloat16)

    @pl.when(jnp.logical_not(has_right))
    def _():
        rims[...] = jnp.zeros_like(rims)
        box_rim[...] = jnp.zeros_like(box_rim)

    peers = merges + jnp.minimum(now, 1) + jnp.minimum(times - 1 - now, 1)
    pl.semaphore_wait(barrier, peers)

    def exchange(m, c):
        return pltpu.make_async_remote_copy(
            src_ref=held.at[0, c], dst_ref=held.at[m + 1, c],
            send_sem=send_sem.at[m, c], recv_sem=recv_sem.at[m, c],
            device_id={"chan": partner[m]}, device_id_type=MESH,
        )

    def rim_copy(m, c):
        slot = (1 - is_upper[m]) * (m + 1)
        return pltpu.make_async_remote_copy(
            src_ref=held.at[slot, c, pl.ds(0, DMAX)], dst_ref=rims.at[m, c],
            send_sem=rim_send.at[m, c], recv_sem=rim_recv.at[m, c],
            device_id={"tm": left}, device_id_type=MESH,
        )

    def box_copy(c):
        return pltpu.make_async_remote_copy(
            src_ref=held.at[0, c, pl.ds(0, 1)], dst_ref=box_rim.at[c],
            send_sem=rim_send.at[merges, c], recv_sem=rim_recv.at[merges, c],
            device_id={"tm": left}, device_id_type=MESH,
        )

    def spill_copy(c):
        return pltpu.make_async_remote_copy(
            src_ref=ext.at[lax.rem(c, 2), pl.ds(0, depth)], dst_ref=spill.at[c],
            send_sem=spill_send.at[c], recv_sem=spill_recv.at[c],
            device_id={"tm": left}, device_id_type=MESH,
        )

    def place(c):
        return c // split, pl.ds(pl.multiple_of(lax.rem(c, split) * per, per), per)

    def result(c):
        return pltpu.make_async_copy(held.at[0, c], out_ref.at[c // split, lax.rem(c, split)], out_sem.at[c])

    def local(c):
        beam = c // split
        q = lax.rem(c, split)
        slot = lax.rem(beam, 2)
        side = lax.rem(c, 2)

        @pl.when(q == 0)
        def _():
            load(beam).wait()

            @pl.when(beam + 1 < beams)
            def _():
                load(beam + 1).start()

        @pl.when(jnp.logical_and(has_left, c >= 2))
        def _():
            spill_copy(c - 2).wait_send()

        ext[side] = jnp.zeros(ext.shape[1:], jnp.float32)
        mat = weight[q]
        group = 4

        def columns(k, carry):
            at = pl.multiple_of(k * (group * TILE), group * TILE)
            part = jnp.dot(mat, fb[slot, :, pl.ds(at, group * TILE)], preferred_element_type=jnp.float32)
            sums = []
            for j in range(group):
                block = part[: shifts * per, j * TILE : (j + 1) * TILE].reshape(shifts, per, TILE)
                ends = [jnp.zeros((n, per, TILE), jnp.float32) for n in (j, group - 1 - j) if n > 0]
                if j > 0:
                    block = jnp.concatenate([ends[0], block], axis=0)
                if j < group - 1:
                    block = jnp.concatenate([block, ends[-1]], axis=0)
                sums.append(block)
            to = pl.ds(k * group, depth + group)
            ext[side, to] = ext[side, to] + ((sums[0] + sums[1]) + (sums[2] + sums[3]))
            return carry

        lax.fori_loop(0, tiles // group, columns, 0, unroll=2)

        @pl.when(has_left)
        def _():
            spill_copy(c).start()

        held[0, c] = ext[side, depth:]

    def join(c):
        @pl.when(has_right)
        def _():
            spill_copy(c).wait_recv()
            held[0, c, tiles - depth :] = held[0, c, tiles - depth :] + spill[c]

        exchange(0, c).start()

    def arrive(m, c):
        exchange(m, c).wait_recv()

        @pl.when(has_left)
        def _():
            rim_copy(m, c).start()

    def merge(m, c):
        exchange(m, c).wait_send()

        @pl.when(has_left)
        def _():
            rim_copy(m, c).wait_send()

        @pl.when(has_right)
        def _():
            rim_copy(m, c).wait_recv()

        low = is_upper[m] * (m + 1)
        high = (1 - is_upper[m]) * (m + 1)
        _, at = place(c)
        lag = lags_of[m, at, :][None]
        last = m == merges - 1
        for start in range(0, tiles, BLOCK):
            end = start + BLOCK
            if end < tiles:
                window = held[high, c, start : end + DMAX]
            else:
                window = jnp.concatenate([held[high, c, start:end], rims[m, c]], axis=0)
            moved = window[:BLOCK]
            for offset in range(1, DMAX + 1):
                moved = jnp.where(lag == float(offset), window[offset : offset + BLOCK], moved)
            new = held[low, c, start:end] + moved
            if last:
                new = new * jnp.float32(1.0 / math.sqrt(CHANS))
            held[0, c, start:end] = new
        if last:
            result(c).start()

            @pl.when(has_left)
            def _():
                box_copy(c).start()
        else:
            exchange(m + 1, c).start()

    def peaks(c):
        @pl.when(has_right)
        def _():
            box_copy(c).wait_recv()

        beam, at = place(c)
        lane = lax.broadcasted_iota(jnp.int32, (per, TILE), 1)
        found = [jnp.zeros((per, TILE), jnp.float32) for _ in range(widths)]
        group = min(16, tiles)
        for first in range(0, tiles, group):
            if first + group < tiles:
                window = held[0, c, first : first + group + 1]
            else:
                window = jnp.concatenate([held[0, c, first : first + group], box_rim[c]], axis=0)
            pairs = jnp.concatenate([window[:group], window[1:]], axis=2).reshape(group * per, 2 * TILE)
            coarse = pairs.astype(jnp.bfloat16)
            fine = (pairs - coarse.astype(jnp.float32)).astype(jnp.bfloat16)
            both = jnp.concatenate([coarse, fine], axis=0)
            sums = jnp.dot(both, band[...], preferred_element_type=jnp.float32)
            sums = sums[: group * per] + sums[group * per :]
            for w in range(widths):
                best = jnp.max(sums[:, w * TILE : (w + 1) * TILE], axis=1, keepdims=True)
                for i in range(group):
                    found[w] = jnp.where(lane == first + i, best[i * per : (i + 1) * per], found[w])
        for w in range(widths):
            span = jnp.full((per, TILE), width_ref[w], jnp.int32).astype(jnp.float32)
            peak_ref[w, beam, at, :] = (found[w] * (1.0 / jnp.sqrt(span)))[:, :tiles]

    lags = [3 + 2 * m for m in range(merges)]
    lags[-1] += 3
    final = lags[-1] + 1

    def step(i, carry):
        def guarded(lag, action):
            c = i - lag

            @pl.when(jnp.logical_and(c >= 0, c < chunks))
            def _():
                action(c)

        for m in reversed(range(merges)):
            guarded(lags[m], functools.partial(arrive, m))
        guarded(1, join)
        guarded(0, local)
        for m in reversed(range(merges)):
            guarded(lags[m], functools.partial(merge, m))
        guarded(final, peaks)
        return carry

    lax.fori_loop(0, chunks + final, step, 0)

    def drain(c, carry):
        result(c).wait()

        @pl.when(has_left)
        def _():
            box_copy(c).wait_send()

            @pl.when(c >= chunks - 2)
            def _():
                spill_copy(c).wait_send()

        return carry

    lax.fori_loop(0, chunks, drain, 0)


def hand_over(series_ref, peak_ref, series_out, peak_out):
    held, split, tiles, per, _ = series_ref.shape
    spans, _, rows, _ = peak_ref.shape
    turned = jnp.swapaxes(peak_ref[...].reshape(spans * held, rows, tiles), 1, 2)
    peak_out[...] = turned.reshape(spans, held, tiles, rows)
    for b in range(held):
        for q in range(split):
            for i in range(tiles):
                series_out[b, q * per : (q + 1) * per, i * TILE : (i + 1) * TILE] = series_ref[b, q, i]


def shards(filterbank, delays, widths):
    beams, chans, length = filterbank.shape
    rows = chans // 4
    per = 8
    chunks = beams * (rows // per)
    local_sections = chans.bit_length() - 1
    merges = lax.axis_size("chan").bit_length() - 1
    times = lax.axis_size("tm")
    tiles = length // TILE
    depth = DMAX * local_sections
    stacked = (depth // 2 + 1) * 2 * per
    sizes = (beams, chans, length, rows, per, merges, times)
    f32 = jnp.float32
    vmem = pl.BlockSpec(memory_space=pltpu.VMEM)
    hbm = pl.BlockSpec(memory_space=pl.ANY)
    dma = pltpu.SemaphoreType.DMA
    split = rows // per
    spans = widths.shape[0]
    shapes = (
        jax.ShapeDtypeStruct((beams, split, tiles, per, TILE), f32),
        jax.ShapeDtypeStruct((spans, beams, rows, tiles), f32),
    )
    results = pl.pallas_call(
        functools.partial(kernel, sizes),
        out_shape=shapes,
        in_specs=[hbm, vmem, pl.BlockSpec(memory_space=pltpu.SMEM)],
        out_specs=(hbm, vmem),
        scratch_shapes=[
            pltpu.VMEM((merges + 1, chunks, tiles, per, TILE), f32),
            pltpu.VMEM((merges, chunks, DMAX, per, TILE), f32),
            pltpu.VMEM((chunks, 1, per, TILE), f32),
            pltpu.VMEM((chunks, depth, per, TILE), f32),
            pltpu.VMEM((2, depth + tiles, per, TILE), f32),
            pltpu.VMEM((rows // per, stacked, chans), jnp.bfloat16),
            pltpu.VMEM((merges, rows, TILE), f32),
            pltpu.VMEM((2 * TILE, widths.shape[0] * TILE), jnp.bfloat16),
            pltpu.VMEM((2, chans, length), jnp.bfloat16),
            dma((merges, chunks)),
            dma((merges, chunks)),
            dma((merges + 1, chunks)),
            dma((merges + 1, chunks)),
            dma((chunks,)),
            dma((chunks,)),
            dma((2,)),
            dma((chunks,)),
        ],
        compiler_params=pltpu.CompilerParams(
            collective_id=0, has_side_effects=True, vmem_limit_bytes=60 * 2**20
        ),
        name="dedisperse",
    )(filterbank, delays, widths)
    series, peaks = pl.pallas_call(
        hand_over,
        grid=(beams // 2,),
        out_shape=(
            jax.ShapeDtypeStruct((beams, rows, length), f32),
            jax.ShapeDtypeStruct((spans, beams, tiles, rows), f32),
        ),
        in_specs=[
            pl.BlockSpec((2, split, tiles, per, TILE), lambda b: (b, 0, 0, 0, 0)),
            pl.BlockSpec((spans, 2, rows, tiles), lambda b: (0, b, 0, 0)),
        ],
        out_specs=(
            pl.BlockSpec((2, rows, length), lambda b: (b, 0, 0)),
            pl.BlockSpec((spans, 2, tiles, rows), lambda b: (0, b, 0, 0)),
        ),
        compiler_params=pltpu.CompilerParams(vmem_limit_bytes=60 * 2**20),
        name="hand_over",
    )(*results)
    return series, jnp.swapaxes(peaks, 2, 3)


def solution(mesh):
    return jax.shard_map(
        shards,
        mesh=mesh,
        in_specs=(P(None, "chan", "tm"), P(None, "chan"), P()),
        out_specs=(P(None, "chan", "tm"), P(None, None, "chan", "tm")),
        check_vma=False,
    )
```
